32 devices in a mesh: lat: 4 (over y, core), lon: 8 (over z, x).
Axes of the slice: x: 2, y: 2, z: 4, core: 2. Of those that a mesh axis runs over, the one named last changes fastest.
Arguments:
- latent: bfloat16 [4, 24, 96, 512], P(None, 'lat', 'lon'), may hold values from -6 to 6
- cotangent: bfloat16 [4, 24, 96, 512], P(None, 'lat', 'lon'), may hold values from -36 to 36
- band_ids: int32 [24], replicated, may hold values from 0 to 5, never falling along the last dimension, each value on 1 to 8 neighbouring positions
- attn_gain: float32 [512], replicated, may hold values from 0.1 to 1.9
- attn_bias: float32 [512], replicated, may hold values from -3 to 3
- ffn_gain: float32 [512], replicated, may hold values from 0.1 to 1.9
- ffn_bias: float32 [512], replicated, may hold values from -3 to 3
- attn_weight: bfloat16 [512, 1536], replicated, may hold values from -26.516504 to 26.516504
- out_weight: bfloat16 [512, 512], replicated, may hold values from -0.25 to 0.25
- up_weight: bfloat16 [512, 1024], replicated, may hold values from -0.25 to 0.25
- down_weight: bfloat16 [1024, 512], replicated, may hold values from -0.1875 to 0.1875
Outputs:
- grad_latent: bfloat16 [4, 24, 96, 512], P(None, 'lat', 'lon')
The draws below stay inside these ranges and needn't reach their ends.
Inputs may be any that keep to these rules, and one draw needn't show every extreme that they name: `band_ids`: never falling along latitude; each band covers 1 to 8 consecutive rows.
All inputs are finite; a program needn't handle non-finite values.
Results may differ from the reference program's by a relative error of at most 0.018.
The reference program's roundings to bfloat16 on the way count: a program that leaves them out, or rounds other values in their place, can miss the bound.
Values may be sent and summed in bfloat16 or wider, within the bound.
A program may use at most 64 MiB of HBM per device.

```python
import math
import jax
import jax.numpy as jnp
import numpy as np
from jax import lax

D = 512
HEADS = 16
MLP = 1024
LEVELS = 4
WIN_LEV = 2
WIN_LAT = 6
WIN_LON = 12
NY = 24
NX = 96


def draw_attn_weight(key, part):
    entries = jnp.clip(jax.random.normal(key, (D, 3 * D), jnp.float32), -6.0, 6.0) * D ** (-0.5)
    return entries.astype(jnp.bfloat16)


def draw_cotangent(key, part):
    lat_pos = jnp.arange(NY, dtype=jnp.float32) / (NY - 1)
    lon_pos = jnp.arange(NX, dtype=jnp.float32) / (NX - 1)
    entries = jnp.clip(jax.random.normal(key, (LEVELS, NY, NX, D), jnp.float32), -4.0, 4.0)
    ramp = jnp.exp(math.log(3.0) * lat_pos)[:, None] * jnp.exp(math.log(3.0) * lon_pos)[None, :]
    return (entries * ramp[None, :, :, None]).astype(jnp.bfloat16)


def shard_levels(stream_key, extent, split, least, largest):
    level = 1.0
    for axis_at, shards_of in split:
        draws = jax.random.uniform(jax.random.fold_in(jax.random.fold_in(stream_key, 6), axis_at), (shards_of,), jnp.float32, least / len(split), largest / len(split))
        level = level * jnp.repeat(jnp.exp(draws), extent[axis_at] // shards_of).reshape((-1,) + (1,) * (len(extent) - 1 - axis_at))
    return level


def length_profile(count, total, limit, slope):
    portions = [(1 << 20) // math.isqrt(standing ** slope) + 1 for standing in range(2, count + 1)]
    surplus, holding = total - limit - (count - 1), [1] * (count - 1)
    while surplus > 0:
        free = [i for i in range(count - 1) if holding[i] < limit]
        whole, budget = sum([portions[i] for i in free]), surplus
        for i in free:
            extra = min(limit - holding[i], max(1, budget * portions[i] // whole), surplus)
            holding[i] = holding[i] + extra
            surplus = surplus - extra
    return np.array([limit] + holding)


def ragged_sizes(key, count, total, limit, skew):
    if count == 2:
        one = jax.random.randint(key, (), max(1, total - limit), min(limit, total - 1) + 1)
        return jnp.stack([one, total - one])
    sizes = jnp.asarray(length_profile(count, total, limit, skew), jnp.int32)
    twos = (count - 1) // 2
    donor, sink = sizes[1:1 + 2 * twos:2], sizes[2:2 + 2 * twos:2]
    slack = jnp.minimum(donor - 1, limit - sink)
    moved = jax.random.randint(jax.random.fold_in(key, 1), (twos,), 0, 1 << 20) % (slack + 1)
    sizes = sizes.at[1:1 + 2 * twos:2].set(donor - moved).at[2:2 + 2 * twos:2].set(sink + moved)
    return sizes[jax.random.permutation(jax.random.fold_in(key, 2), count)]


def gaussian(stream_key, dims, scale, limit, cuts=(), kind=jnp.bfloat16):
    level = shard_levels(stream_key, dims, cuts, -0.22, 0.18) if cuts else 1.0
    array = jax.random.normal(stream_key, dims, jnp.float32) * scale * level
    return jnp.minimum(jnp.maximum(array, -limit), limit).astype(kind)


def setup_inputs(seed: int = 0) -> dict:
    splits = jax.random.split(jax.random.key(seed), 12)
    return {
        "latent": gaussian(splits[0], (LEVELS, NY, NX, D), 1.0, 6.0, ((1, 4), (2, 8))),
        "cotangent": draw_cotangent(jax.random.fold_in(splits[11], 71), 0),
        "band_ids": jnp.searchsorted(jnp.cumsum(ragged_sizes(splits[2], NY // 4, NY, 8, 0)), jnp.arange(NY), side="right").astype(jnp.int32),
        "attn_gain": jnp.clip(1.0 + 0.18 * jax.random.normal(splits[3], (D,), jnp.float32), 0.1, 1.9),
        "attn_bias": gaussian(splits[4], (D,), 0.5, 3.0, (), jnp.float32),
        "ffn_gain": jnp.clip(1.0 + 0.18 * jax.random.normal(splits[5], (D,), jnp.float32), 0.1, 1.9),
        "ffn_bias": gaussian(splits[6], (D,), 0.5, 3.0, (), jnp.float32),
        "attn_weight": draw_attn_weight(jax.random.fold_in(splits[11], 71), 0),
        "out_weight": gaussian(splits[8], (D, D), D ** -0.5, 0.25),
        "up_weight": gaussian(splits[9], (D, MLP), D ** -0.5, 0.25),
        "down_weight": gaussian(splits[10], (MLP, D), MLP ** -0.5, 0.1875),
    }


SQRT_HALF = 0.7071067811865476
INV_SQRT_TAU = 0.3989422804014327
clip_level = 0.2

def normalize(values):
    center = values - lax.optimization_barrier(jnp.mean(values, axis=-1, keepdims=True))
    inv_scale = lax.rsqrt(lax.optimization_barrier(jnp.mean(center * center, axis=-1, keepdims=True)) + 1e-05)
    return (center * inv_scale, inv_scale)

def norm_back(normed, inv_scale, gain, grad_norm):
    scaled = grad_norm * gain
    return inv_scale * (scaled - lax.optimization_barrier(jnp.mean(scaled, axis=-1, keepdims=True)) - normed * lax.optimization_barrier(jnp.mean(scaled * normed, axis=-1, keepdims=True)))

def product(form, left, right):
    return jnp.einsum(form, left.astype(jnp.float32), right.astype(jnp.float32), precision=lax.Precision.HIGHEST)

def to_windows(blocks):
    level_count, row_count, column_count, channel_count = blocks.shape
    shaped = blocks.reshape(level_count // WIN_LEV, WIN_LEV, row_count // WIN_LAT, WIN_LAT, column_count // WIN_LON, WIN_LON, channel_count)
    return shaped.transpose(0, 2, 4, 1, 3, 5, 6).reshape(-1, WIN_LEV * WIN_LAT * WIN_LON, channel_count)

def from_windows(windows, level_count, row_count, column_count):
    channel_count = windows.shape[-1]
    shaped = windows.reshape(level_count // WIN_LEV, row_count // WIN_LAT, column_count // WIN_LON, WIN_LEV, WIN_LAT, WIN_LON, channel_count)
    return shaped.transpose(0, 3, 1, 4, 2, 5, 6).reshape(level_count, row_count, column_count, channel_count)

def attend_forward(windows_in, labels, attn_gain, attn_bias, attn_weight, out_weight):
    window_count, window_size, width = windows_in.shape
    head_size = width // HEADS
    score_scale = head_size ** (-0.5)
    flat_in = windows_in.reshape(-1, width).astype(jnp.float32)
    normed, inv_scale = normalize(flat_in)
    hidden_in = (normed * attn_gain + attn_bias).astype(jnp.bfloat16)
    projected = jnp.dot(hidden_in, attn_weight, preferred_element_type=jnp.float32).astype(jnp.bfloat16)
    projected = projected.reshape(window_count, window_size, 3, HEADS, head_size)
    query_rows = projected[:, :, 0]
    key_rows = projected[:, :, 1]
    value_rows = projected[:, :, 2]
    scores = product('wqhe,wkhe->whqk', query_rows, key_rows) * score_scale
    allowed = labels[:, None, :, None] == labels[:, None, None, :]
    scores = jnp.where(allowed, scores, -jnp.inf)
    row_max = lax.optimization_barrier(jnp.max(scores, axis=-1, keepdims=True))
    expo_terms = jnp.exp(scores - row_max)
    attn_probs = expo_terms / lax.optimization_barrier(jnp.sum(expo_terms, axis=-1, keepdims=True))
    rounded_probs = attn_probs.astype(jnp.bfloat16)
    mixed_heads = product('whqk,wkhe->wqhe', rounded_probs, value_rows).astype(jnp.bfloat16).reshape(-1, width)
    residual = flat_in + jnp.dot(mixed_heads, out_weight, preferred_element_type=jnp.float32)
    return (residual, (normed, inv_scale, query_rows, key_rows, value_rows, attn_probs, rounded_probs))

def feed_backward(residual, cotangent_rows, ffn_gain, ffn_bias, up_weight, down_weight):
    normed, inv_scale = normalize(residual)
    hidden_in = (normed * ffn_gain + ffn_bias).astype(jnp.bfloat16)
    pre_act = jnp.dot(hidden_in, up_weight, preferred_element_type=jnp.float32)
    grad_act = jnp.dot(cotangent_rows, down_weight.T, preferred_element_type=jnp.float32)
    gelu_slope = 0.5 * (1.0 + jax.scipy.special.erf(pre_act * SQRT_HALF)) + pre_act * jnp.exp(-0.5 * pre_act * pre_act) * INV_SQRT_TAU
    grad_pre = (grad_act * gelu_slope).astype(jnp.bfloat16)
    grad_hidden = jnp.dot(grad_pre, up_weight.T, preferred_element_type=jnp.float32)
    return cotangent_rows.astype(jnp.float32) + norm_back(normed, inv_scale, ffn_gain, grad_hidden)

def attend_backward(grad_resid, cached, attn_gain, attn_weight, out_weight):
    normed, inv_scale, query_rows, key_rows, value_rows, attn_probs, rounded_probs = cached
    window_count, window_size, head_count, head_size = query_rows.shape
    score_scale = head_size ** (-0.5)
    grad_mixed = jnp.dot(grad_resid.astype(jnp.bfloat16), out_weight.T, preferred_element_type=jnp.float32).astype(jnp.bfloat16)
    grad_mixed = grad_mixed.reshape(window_count, window_size, head_count, head_size)
    grad_probs = product('wqhe,wkhe->whqk', grad_mixed, value_rows)
    grad_value = product('whqk,wqhe->wkhe', rounded_probs, grad_mixed).astype(jnp.bfloat16)
    grad_scores = (attn_probs * (grad_probs - lax.optimization_barrier(jnp.sum(attn_probs * grad_probs, axis=-1, keepdims=True))) * score_scale).astype(jnp.bfloat16)
    grad_query = product('whqk,wkhe->wqhe', grad_scores, key_rows).astype(jnp.bfloat16)
    grad_key = product('whqk,wqhe->wkhe', grad_scores, query_rows).astype(jnp.bfloat16)
    grad_proj = jnp.stack([grad_query, grad_key, grad_value], axis=2).reshape(-1, 3 * head_count * head_size)
    grad_hidden = jnp.dot(grad_proj, attn_weight.T, preferred_element_type=jnp.float32)
    return norm_back(normed, inv_scale, attn_gain, grad_hidden)

def reference(latent, cotangent, band_ids, attn_gain, attn_bias, ffn_gain, ffn_bias, attn_weight, out_weight, up_weight, down_weight):
    half_lat = WIN_LAT // 2
    half_lon = WIN_LON // 2
    shifted = jnp.roll(latent, (-1, -half_lat, -half_lon), axis=(0, 1, 2))
    cot_shift = jnp.roll(cotangent, (-1, -half_lat, -half_lon), axis=(0, 1, 2))
    row_bands = jnp.roll(band_ids, -half_lat)
    flags = ((jnp.arange(LEVELS, dtype=jnp.int32) + 1) % LEVELS == 0).astype(jnp.int32)
    label_rows = 2 * row_bands[None, :] + flags[:, None]
    label_grid = jnp.broadcast_to(label_rows[:, :, None, None], (LEVELS, NY, NX, 1))
    windows_in = to_windows(shifted)
    grad_windows = to_windows(cot_shift)
    label_windows = to_windows(label_grid)[:, :, 0]
    window_size = WIN_LEV * WIN_LAT * WIN_LON
    batch_count = NX // WIN_LON
    group_count = windows_in.shape[0] // batch_count

    def one_group(items):
        group_in, group_grad, group_labels = items
        residual, cached = attend_forward(group_in, group_labels, attn_gain, attn_bias, attn_weight, out_weight)
        grad_resid = feed_backward(residual, group_grad.reshape(-1, D), ffn_gain, ffn_bias, up_weight, down_weight)
        grad_shift = grad_resid + attend_backward(grad_resid, cached, attn_gain, attn_weight, out_weight)
        return grad_shift.reshape(group_in.shape)
    result = lax.map(one_group, (windows_in.reshape(group_count, batch_count, window_size, D), grad_windows.reshape(group_count, batch_count, window_size, D), label_windows.reshape(group_count, batch_count, window_size)))
    grad_shift = from_windows(result.reshape(-1, window_size, D), LEVELS, NY, NX)
    grad_full = jnp.roll(grad_shift, (1, half_lat, half_lon), axis=(0, 1, 2))
    total = jnp.sum(grad_full * grad_full)
    clip = jnp.minimum(1.0, clip_level * lax.rsqrt(total / (LEVELS * NY * NX * D) + 1e-06))
    return (grad_full * clip).astype(jnp.bfloat16)
```

```python
import functools

import jax
import jax.numpy as jnp
from jax import lax
from jax.experimental import pallas as pl
from jax.experimental.pallas import tpu as pltpu
from jax.sharding import PartitionSpec as P

HEADS = 16
WIN_LEV = 2
WIN_LAT = 6
WIN_LON = 12

SQRT_HALF = 0.7071067811865476
INV_SQRT_TAU = 0.3989422804014327
LOG2_E = 1.4426950408889634
CLIP_LEVEL = 0.2
MESH = pl.DeviceIdType.MESH
F32 = jnp.float32
BF16 = jnp.bfloat16


def dot(a, b, dims=((1,), (0,))):
    return lax.dot_general(a, b, (dims, ((), ())), preferred_element_type=F32)


def normalize(values):
    center = values - jnp.mean(values, axis=-1, keepdims=True)
    inv_scale = lax.rsqrt(jnp.mean(center * center, axis=-1, keepdims=True) + 1e-05)
    return center * inv_scale, inv_scale


def norm_back(normed, inv_scale, gain, grad_norm):
    scaled = grad_norm * gain
    return inv_scale * (
        scaled
        - jnp.mean(scaled, axis=-1, keepdims=True)
        - normed * jnp.mean(scaled * normed, axis=-1, keepdims=True)
    )


class Layout:
    def __init__(self, shape, n_lat, n_lon):
        self.levels, self.rows, self.cols, self.width = shape
        assert self.rows == WIN_LAT and self.cols == WIN_LON
        self.n_lat, self.n_lon = n_lat, n_lon
        self.hr, self.hc = self.rows // 2, self.cols // 2
        self.wins = self.levels // WIN_LEV
        self.part = WIN_LEV * self.hr * self.hc
        self.size = 4 * self.part
        self.quad = self.wins * self.part
        self.back = -(-self.quad // 16) * 16

    def place(self, level, row):
        shifted = (level - 1) % self.levels
        half = 0 if row >= self.hr else 1
        return half, (shifted * self.hr + row % self.hr) * self.hc


def mask_bias(lay, window, band_ref, row_start):
    total = band_ref.shape[0]
    bands = [band_ref[lax.rem(row_start + r + lay.hr, total)] for r in range(lay.rows)]

    def labels(dim):
        cell = lax.broadcasted_iota(jnp.int32, (lay.size, lay.size), dim)
        quad = jnp.zeros_like(cell)
        for i in range(1, 4):
            quad += (cell >= i * lay.part).astype(jnp.int32)
        cell = cell - quad * lay.part
        level = jnp.zeros_like(cell)
        for i in range(1, WIN_LEV):
            level += (cell >= i * lay.hr * lay.hc).astype(jnp.int32)
        cell = cell - level * (lay.hr * lay.hc)
        row = jnp.zeros_like(cell)
        for i in range(1, lay.hr):
            row += (cell >= i * lay.hc).astype(jnp.int32)
        row = row + (quad >= 2).astype(jnp.int32) * lay.hr
        label = jnp.zeros_like(cell)
        for r in range(lay.rows):
            label = jnp.where(row == r, 2 * bands[r], label)
        last = level + window * WIN_LEV == lay.levels - 1
        return label + last.astype(jnp.int32)

    return jnp.where(labels(0) == labels(1), 0.0, -jnp.inf).astype(F32)


def kernel(
    lay,
    latent_hbm, cotangent_hbm, band_ref, ag_ref, ab_ref, fg_ref, fb_ref,
    wqkv_hbm, wout_hbm, wup_hbm, wdown_hbm,
    out_ref,
    latent_v, cotangent_v, wqkv, wout, wup, wdown,
    pack, sent, landed, xs, cs, n1_s, bias, qkv_t, probs, mix_t, gm_t, gqkv_t,
    grad_s, back_out, back_in, sums_lat, sums_lon,
    load_sem, send_sem, recv_sem, bsend_sem, brecv_sem,
    lat_send, lat_recv, lon_send, lon_recv,
):
    lat, lon = lax.axis_index("lat"), lax.axis_index("lon")
    nl, nn = lay.n_lat, lay.n_lon
    width, part, quad, size, wins = lay.width, lay.part, lay.quad, lay.size, lay.wins
    head = width // HEADS

    def at(dlat, dlon):
        return {"lat": lax.rem(lat + dlat + nl, nl), "lon": lax.rem(lon + dlon + nn, nn)}

    barrier = pltpu.get_barrier_semaphore()
    peers = [at(k, 0) for k in range(1, nl)] + [at(0, k) for k in range(1, nn)]
    peers += [at(1, 1), at(-1, -1)]
    for peer in peers:
        pl.semaphore_signal(barrier, inc=1, device_id=peer, device_id_type=MESH)

    loads = [
        pltpu.make_async_copy(src, dst, load_sem.at[i])
        for i, (src, dst) in enumerate([
            (latent_hbm, latent_v), (cotangent_hbm, cotangent_v), (wqkv_hbm, wqkv),
            (wdown_hbm, wdown), (wout_hbm, wout), (wup_hbm, wup),
        ])
    ]
    for load in loads:
        load.start()

    loads[0].wait()
    loads[1].wait()
    for which, block in enumerate((latent_v, cotangent_v)):
        for level in range(lay.levels):
            for row in range(lay.rows):
                half, first = lay.place(level, row)
                cells = block[level, row].astype(F32)
                to = pl.ds(which * quad + first, lay.hc)
                pack[2 * half, to] = cells[lay.hc:]
                pack[2 * half + 1, to] = cells[: lay.hc]
    for q in range(1, 4):
        sent[q - 1] = pack[q].astype(BF16)
    pl.semaphore_wait(barrier, len(peers))
    moves = [
        pltpu.make_async_remote_copy(
            src_ref=sent.at[q - 1], dst_ref=landed.at[q - 1],
            send_sem=send_sem.at[q - 1], recv_sem=recv_sem.at[q - 1],
            device_id=at(-(q // 2), -(q % 2)), device_id_type=MESH,
        )
        for q in range(1, 4)
    ]
    for move in moves:
        move.start()

    for w in range(wins):
        bias[w] = mask_bias(lay, w, band_ref, lat * lay.rows)

    for q in (0, 2, 1, 3):
        if q:
            moves[q - 1].wait()
            cells = landed[q - 1].astype(F32)
        else:
            cells = pack[0]
        for w in range(wins):
            to = pl.ds(w * size + q * part, part)
            xs[to] = cells[w * part : (w + 1) * part]
            cs[to] = cells[quad + w * part : quad + (w + 1) * part]

    n1, r1 = normalize(xs[...])
    n1_s[...] = n1
    h1 = (n1 * ag_ref[...] + ab_ref[...]).astype(BF16)
    loads[2].wait()
    for c in range(3):
        columns = slice(c * width, (c + 1) * width)
        qkv = dot(h1, wqkv[:, columns])
        for w in range(wins):
            qkv_t[w, columns] = qkv[w * size : (w + 1) * size].T.astype(BF16)

    scale = head ** (-0.5)
    unroll = 2

    def parts_of(w, h):
        def rows(block):
            return pl.ds(pl.multiple_of(block * width + h * head, head), head)

        return [qkv_t[w, rows(b)] for b in range(3)]

    def ahead(step, carry):
        for u in range(unroll):
            h = step * unroll + u
            for w in range(wins):
                q_t, k_t, v_t = parts_of(w, h)
                scores = dot(k_t, q_t, ((0,), (0,))) + bias[w]
                top = jnp.max(scores, axis=0, keepdims=True)
                expo = jnp.exp2((scores - top) * (scale * LOG2_E))
                p = expo * (1.0 / jnp.sum(expo, axis=0, keepdims=True))
                probs[h * wins + w] = p
                mix_t[w, pl.ds(pl.multiple_of(h * head, head), head)] = dot(v_t, p.astype(BF16))
        return carry

    lax.fori_loop(0, HEADS // unroll, ahead, 0)

    loads[3].wait()
    loads[4].wait()
    loads[5].wait()
    mixed = jnp.concatenate([mix_t[w].T.astype(BF16) for w in range(wins)], axis=0)
    resid = xs[...] + dot(mixed, wout[...])

    n2, r2 = normalize(resid)
    h2 = (n2 * fg_ref[...] + fb_ref[...]).astype(BF16)
    cot = cs[...].astype(BF16)
    hidden = wup.shape[1]
    chunk = min(256, hidden)
    grad_h2 = None
    for c in range(0, hidden, chunk):
        pre = dot(h2, wup[:, c : c + chunk])
        act = dot(cot, wdown[c : c + chunk], ((1,), (1,)))
        slope = 0.5 * (1.0 + lax.erf(pre * SQRT_HALF)) + pre * jnp.exp(-0.5 * pre * pre) * INV_SQRT_TAU
        grad_pre = (act * slope).astype(BF16)
        term = dot(grad_pre, wup[:, c : c + chunk], ((1,), (1,)))
        grad_h2 = term if grad_h2 is None else grad_h2 + term
    grad_resid = cs[...] + norm_back(n2, r2, fg_ref[...], grad_h2)
    grad_s[...] = grad_resid
    grad_r = grad_resid.astype(BF16)
    for w in range(wins):
        gm_t[w] = dot(wout[...], grad_r[w * size : (w + 1) * size], ((1,), (1,))).astype(BF16)

    def behind(step, carry):
        for u in range(unroll):
            h = step * unroll + u
            mine = pl.ds(pl.multiple_of(h * head, head), head)
            for w in range(wins):
                q_t, k_t, v_t = parts_of(w, h)
                g_t = gm_t[w, mine]
                p = probs[h * wins + w]
                grad_p = dot(v_t, g_t, ((0,), (0,)))
                inner = jnp.sum(p * grad_p, axis=0, keepdims=True)
                grad_sc = (p * (grad_p - inner) * scale).astype(BF16)
                grads = (
                    dot(k_t, grad_sc),
                    dot(q_t, grad_sc, ((1,), (1,))),
                    dot(g_t, p.astype(BF16), ((1,), (1,))),
                )
                for b in range(3):
                    rows = pl.ds(pl.multiple_of(b * width + h * head, head), head)
                    gqkv_t[w, rows] = grads[b].astype(BF16)
        return carry

    lax.fori_loop(0, HEADS // unroll, behind, 0)

    grad_h1 = jnp.concatenate([dot(wqkv[...], gqkv_t[w]).T for w in range(wins)], axis=0)
    grad = grad_s[...] + norm_back(n1_s[...], r1, ag_ref[...], grad_h1)
    grad_s[...] = grad

    squares = jnp.sum((grad * grad).reshape(-1, 8, width), axis=0)
    tile = functools.reduce(jnp.add, [squares[:, c : c + 128] for c in range(0, width, 128)])

    def exchange(buffer, own, count, send, recv, peer):
        buffer[0] = own
        copies = [
            pltpu.make_async_remote_copy(
                src_ref=buffer.at[0], dst_ref=buffer.at[k],
                send_sem=send.at[k], recv_sem=recv.at[k],
                device_id=peer(k), device_id_type=MESH,
            )
            for k in range(1, count)
        ]
        for copy in copies:
            copy.start()
        return copies

    lat_copies = exchange(sums_lat, tile, nl, lat_send, lat_recv, lambda k: at(k, 0))

    returns = []
    for q in range(3, -1, -1):
        for w in range(wins):
            pack[q, pl.ds(w * part, part)] = grad_s[pl.ds(w * size + q * part, part)]
        if q:
            back_out[q - 1] = pack[q, : lay.back].astype(BF16)
            returns.append(pltpu.make_async_remote_copy(
                src_ref=back_out.at[q - 1], dst_ref=back_in.at[q - 1],
                send_sem=bsend_sem.at[q - 1], recv_sem=brecv_sem.at[q - 1],
                device_id=at(q // 2, q % 2), device_id_type=MESH,
            ))
            returns[-1].start()

    for copy in lat_copies:
        copy.wait()
    lat_sum = jnp.sum(sums_lat[...], axis=0)
    lon_copies = exchange(sums_lon, lat_sum, nn, lon_send, lon_recv, lambda k: at(0, k))
    for move in returns:
        move.wait()
    for copy in lon_copies:
        copy.wait()
    total = jnp.sum(jnp.sum(sums_lon[...], axis=0), keepdims=True)
    entries = wins * size * width * nl * nn
    clip = jnp.minimum(1.0, CLIP_LEVEL * lax.rsqrt(total / entries + 1e-06))

    quads = [pack[0, :quad]] + [back_in[q, :].astype(F32)[:quad] for q in range(3)]
    quads = [cells * clip for cells in quads]
    for level in range(lay.levels):
        for row in range(lay.rows):
            half, first = lay.place(level, row)
            near = quads[2 * half + 1][first : first + lay.hc]
            far = quads[2 * half][first : first + lay.hc]
            out_ref[level, row] = jnp.concatenate([near, far], axis=0).astype(BF16)


def solution(mesh):
    n_lat, n_lon = mesh.shape["lat"], mesh.shape["lon"]

    def shards(
        latent, cotangent, band_ids, attn_gain, attn_bias, ffn_gain, ffn_bias,
        attn_weight, out_weight, up_weight, down_weight,
    ):
        lay = Layout(latent.shape, n_lat, n_lon)
        width, tokens = lay.width, lay.wins * lay.size
        hbm = pl.BlockSpec(memory_space=pl.ANY)
        vmem = pl.BlockSpec(memory_space=pltpu.VMEM)
        smem = pl.BlockSpec(memory_space=pltpu.SMEM)
        dma = pltpu.SemaphoreType.DMA
        scratch = [
            pltpu.VMEM(latent.shape, BF16), pltpu.VMEM(cotangent.shape, BF16),
            pltpu.VMEM(attn_weight.shape, BF16), pltpu.VMEM(out_weight.shape, BF16),
            pltpu.VMEM(up_weight.shape, BF16), pltpu.VMEM(down_weight.shape, BF16),
            pltpu.VMEM((4, 2 * lay.quad, width), F32),
            pltpu.VMEM((3, 2 * lay.quad, width), BF16),
            pltpu.VMEM((3, 2 * lay.quad, width), BF16),
            pltpu.VMEM((tokens, width), F32),
            pltpu.VMEM((tokens, width), F32),
            pltpu.VMEM((tokens, width), F32),
            pltpu.VMEM((lay.wins, lay.size, lay.size), F32),
            pltpu.VMEM((lay.wins, 3 * width, lay.size), BF16),
            pltpu.VMEM((lay.wins * HEADS, lay.size, lay.size), F32),
            pltpu.VMEM((lay.wins, width, lay.size), F32),
            pltpu.VMEM((lay.wins, width, lay.size), BF16),
            pltpu.VMEM((lay.wins, 3 * width, lay.size), BF16),
            pltpu.VMEM((tokens, width), F32),
            pltpu.VMEM((3, lay.back, width), BF16),
            pltpu.VMEM((3, lay.back, width), BF16),
            pltpu.VMEM((n_lat, 8, 128), F32),
            pltpu.VMEM((n_lon, 8, 128), F32),
            dma((6,)), dma((3,)), dma((3,)), dma((3,)), dma((3,)),
            dma((n_lat,)), dma((n_lat,)), dma((n_lon,)), dma((n_lon,)),
        ]
        return pl.pallas_call(
            functools.partial(kernel, lay),
            out_shape=jax.ShapeDtypeStruct(latent.shape, BF16),
            in_specs=[hbm, hbm, smem, vmem, vmem, vmem, vmem, hbm, hbm, hbm, hbm],
            out_specs=vmem,
            scratch_shapes=scratch,
            compiler_params=pltpu.CompilerParams(
                collective_id=0, has_side_effects=True, vmem_limit_bytes=48 * 2**20
            ),
        )(
            latent, cotangent, band_ids,
            attn_gain.reshape(1, width), attn_bias.reshape(1, width),
            ffn_gain.reshape(1, width), ffn_bias.reshape(1, width),
            attn_weight, out_weight, up_weight, down_weight,
        )

    block = P(None, "lat", "lon", None)
    return jax.shard_map(
        shards, mesh=mesh, in_specs=(block, block) + (P(),) * 9, out_specs=block, check_vma=False
    )
```

```python
import functools

import jax
import jax.numpy as jnp
from jax import lax
from jax.experimental import pallas as pl
from jax.experimental.pallas import tpu as pltpu
from jax.sharding import PartitionSpec as P

HEADS = 16
WIN_LEV = 2
WIN_LAT = 6
WIN_LON = 12

SQRT_HALF = 0.7071067811865476
INV_SQRT_TAU = 0.3989422804014327
LOG2_E = 1.4426950408889634
CLIP_LEVEL = 0.2
MESH = pl.DeviceIdType.MESH
F32 = jnp.float32
BF16 = jnp.bfloat16


def dot(a, b, dims=((1,), (0,))):
    return lax.dot_general(a, b, (dims, ((), ())), preferred_element_type=F32)


def normalize(values):
    center = values - jnp.mean(values, axis=-1, keepdims=True)
    inv_scale = lax.rsqrt(jnp.mean(center * center, axis=-1, keepdims=True) + 1e-05)
    return center * inv_scale, inv_scale


def norm_back(normed, inv_scale, gain, grad_norm):
    scaled = grad_norm * gain
    return inv_scale * (
        scaled
        - jnp.mean(scaled, axis=-1, keepdims=True)
        - normed * jnp.mean(scaled * normed, axis=-1, keepdims=True)
    )


class Layout:
    def __init__(self, shape, n_lat, n_lon):
        self.rows, self.cols, self.levels, self.width = shape
        assert self.rows == WIN_LAT and self.cols == WIN_LON
        self.n_lat, self.n_lon = n_lat, n_lon
        self.hr, self.hc = self.rows // 2, self.cols // 2
        self.wins = self.levels // WIN_LEV
        self.plane = self.rows * self.cols
        self.size = WIN_LEV * self.plane
        self.quad = self.plane // 4 * self.levels

    def source(self, q):
        row, col = (0 if q // 2 else self.hr), (0 if q % 2 else self.hc)
        return pl.ds(row, self.hr), pl.ds(col, self.hc)


def mask_bias(lay, window, band_ref, row_start):
    total = band_ref.shape[0]
    bands = [band_ref[lax.rem(row_start + r + lay.hr, total)] for r in range(lay.rows)]

    def labels(dim):
        cell = lax.broadcasted_iota(jnp.int32, (lay.size, lay.size), dim)
        level = jnp.zeros_like(cell)
        for i in range(1, WIN_LEV):
            level += (cell >= i * lay.plane).astype(jnp.int32)
        cell = cell - level * lay.plane
        half = (cell >= lay.plane // 2).astype(jnp.int32)
        cell = cell - half * (lay.plane // 2)
        cell = cell - (cell >= lay.plane // 4).astype(jnp.int32) * (lay.plane // 4)
        row = half * lay.hr
        for i in range(1, lay.hr):
            row += (cell >= i * lay.hc).astype(jnp.int32)
        label = jnp.zeros_like(cell)
        for r in range(lay.rows):
            label = jnp.where(row == r, 2 * bands[r], label)
        last = level + window * WIN_LEV == lay.levels - 1
        return label + last.astype(jnp.int32)

    return jnp.where(labels(0) == labels(1), 0.0, -jnp.inf).astype(F32)


def kernel(
    lay,
    latent_hbm, cotangent_hbm, band_hbm, ag_hbm, ab_hbm, fg_hbm, fb_hbm,
    wqkv_hbm, wout_hbm, wup_hbm, wdown_hbm,
    out_ref,
    band_ref, ag_ref, ab_ref, fg_ref, fb_ref, wqkv, wout, wup, wdown,
    landed, stage, xs, cs, n1_s, bias, qkv_t, probs, mix_t, gm_t, gqkv_t,
    grad_s, back_out, back_in, sums_lat, sums_lon,
    load_sem, own_sem, send_sem, recv_sem, bsend_sem, brecv_sem,
    lat_send, lat_recv, lon_send, lon_recv,
):
    lat, lon = lax.axis_index("lat"), lax.axis_index("lon")
    nl, nn = lay.n_lat, lay.n_lon
    width, quad, size, wins = lay.width, lay.quad, lay.size, lay.wins
    head = width // HEADS

    def at(dlat, dlon):
        return {"lat": lax.rem(lat + dlat + nl, nl), "lon": lax.rem(lon + dlon + nn, nn)}

    barrier = pltpu.get_barrier_semaphore()
    peers = [at(k, 0) for k in range(1, nl)] + [at(0, k) for k in range(1, nn)]
    peers += [at(1, 1), at(-1, -1)]
    for peer in peers:
        pl.semaphore_signal(barrier, inc=1, device_id=peer, device_id_type=MESH)

    blocks = (latent_hbm, cotangent_hbm)
    owns = [
        pltpu.make_async_copy(block.at[lay.source(0)], landed.at[i, 0], own_sem.at[i])
        for i, block in enumerate(blocks)
    ]
    loads = [
        pltpu.make_async_copy(src, dst, load_sem.at[i])
        for i, (src, dst) in enumerate([
            (band_hbm, band_ref), (ag_hbm, ag_ref), (ab_hbm, ab_ref), (wqkv_hbm, wqkv),
            (wdown_hbm, wdown), (wout_hbm, wout), (wup_hbm, wup), (fg_hbm, fg_ref), (fb_hbm, fb_ref),
        ])
    ]
    for load in owns + loads:
        load.start()

    pl.semaphore_wait(barrier, len(peers))
    moves = [
        pltpu.make_async_remote_copy(
            src_ref=block.at[lay.source(q)], dst_ref=landed.at[i, q],
            send_sem=send_sem.at[i, q], recv_sem=recv_sem.at[i, q],
            device_id=at(-(q // 2), -(q % 2)), device_id_type=MESH,
        )
        for i, block in enumerate(blocks)
        for q in (3, 2, 1)
    ]
    for move in moves:
        move.start()

    loads[0].wait()
    for w in range(wins):
        bias[w] = mask_bias(lay, w, band_ref, lat * lay.rows)

    chunks = [(c, slice(c * 128, (c + 1) * 128)) for c in range(width // 128)]

    def levels(w):
        for lev in range(WIN_LEV):
            level = (w * WIN_LEV + lev + 1) % lay.levels
            rows = pl.ds((w * WIN_LEV + lev) * lay.plane, lay.plane)
            yield rows, pl.ds(level, lay.plane, stride=lay.levels)

    for i, kept in enumerate((xs, cs)):
        owns[i].wait()
        for move in moves[3 * i : 3 * i + 3]:
            move.wait()
        for q in range(4):
            cells = landed[i, q].astype(F32).reshape(quad, width)
            for c, lanes in chunks:
                stage[c, pl.ds(q * quad, quad)] = cells[:, lanes]
        for w in range(wins):
            for rows, spread in levels(w):
                for c, lanes in chunks:
                    kept[rows, lanes] = stage[c, spread]

    loads[1].wait()
    loads[2].wait()
    n1, r1 = normalize(xs[...])
    n1_s[...] = n1
    h1 = (n1 * ag_ref[...] + ab_ref[...]).astype(BF16)
    loads[3].wait()
    for c in range(3):
        columns = slice(c * width, (c + 1) * width)
        qkv = dot(h1, wqkv[:, columns])
        for w in range(wins):
            qkv_t[w, columns] = qkv[w * size : (w + 1) * size].T.astype(BF16)

    scale = head ** (-0.5)
    unroll = 2

    def parts_of(w, h):
        def rows(block):
            return pl.ds(pl.multiple_of(block * width + h * head, head), head)

        return [qkv_t[w, rows(b)] for b in range(3)]

    def ahead(step, carry):
        for u in range(unroll):
            h = step * unroll + u
            for w in range(wins):
                q_t, k_t, v_t = parts_of(w, h)
                scores = dot(k_t, q_t, ((0,), (0,))) + bias[w]
                top = jnp.max(scores, axis=0, keepdims=True)
                expo = jnp.exp2((scores - top) * (scale * LOG2_E))
                p = expo * (1.0 / jnp.sum(expo, axis=0, keepdims=True))
                probs[h * wins + w] = p
                mix_t[w, pl.ds(pl.multiple_of(h * head, head), head)] = dot(v_t, p.astype(BF16))
        return carry

    lax.fori_loop(0, HEADS // unroll, ahead, 0)

    for load in loads[4:]:
        load.wait()
    mixed = jnp.concatenate([mix_t[w].T.astype(BF16) for w in range(wins)], axis=0)
    resid = xs[...] + dot(mixed, wout[...])

    n2, r2 = normalize(resid)
    h2 = (n2 * fg_ref[...] + fb_ref[...]).astype(BF16)
    cot = cs[...].astype(BF16)
    hidden = wup.shape[1]
    chunk = min(256, hidden)
    grad_h2 = None
    for c in range(0, hidden, chunk):
        pre = dot(h2, wup[:, c : c + chunk])
        act = dot(cot, wdown[c : c + chunk], ((1,), (1,)))
        slope = 0.5 * (1.0 + lax.erf(pre * SQRT_HALF)) + pre * jnp.exp(-0.5 * pre * pre) * INV_SQRT_TAU
        grad_pre = (act * slope).astype(BF16)
        term = dot(grad_pre, wup[:, c : c + chunk], ((1,), (1,)))
        grad_h2 = term if grad_h2 is None else grad_h2 + term
    grad_resid = cs[...] + norm_back(n2, r2, fg_ref[...], grad_h2)
    grad_s[...] = grad_resid
    grad_r = grad_resid.astype(BF16)
    for w in range(wins):
        gm_t[w] = dot(wout[...], grad_r[w * size : (w + 1) * size], ((1,), (1,))).astype(BF16)

    def behind(step, carry):
        for u in range(unroll):
            h = step * unroll + u
            mine = pl.ds(pl.multiple_of(h * head, head), head)
            for w in range(wins):
                q_t, k_t, v_t = parts_of(w, h)
                g_t = gm_t[w, mine]
                p = probs[h * wins + w]
                grad_p = dot(v_t, g_t, ((0,), (0,)))
                inner = jnp.sum(p * grad_p, axis=0, keepdims=True)
                grad_sc = (p * (grad_p - inner) * scale).astype(BF16)
                grads = (
                    dot(k_t, grad_sc),
                    dot(q_t, grad_sc, ((1,), (1,))),
                    dot(g_t, p.astype(BF16), ((1,), (1,))),
                )
                for b in range(3):
                    rows = pl.ds(pl.multiple_of(b * width + h * head, head), head)
                    gqkv_t[w, rows] = grads[b].astype(BF16)
        return carry

    lax.fori_loop(0, HEADS // unroll, behind, 0)

    grad_h1 = jnp.concatenate([dot(wqkv[...], gqkv_t[w]).T for w in range(wins)], axis=0)
    grad = grad_s[...] + norm_back(n1_s[...], r1, ag_ref[...], grad_h1)
    grad_s[...] = grad

    squares = jnp.sum((grad * grad).reshape(-1, 8, width), axis=0)
    tile = functools.reduce(jnp.add, [squares[:, c : c + 128] for c in range(0, width, 128)])

    def exchange(buffer, own, count, send, recv, peer):
        buffer[0] = own
        copies = [
            pltpu.make_async_remote_copy(
                src_ref=buffer.at[0], dst_ref=buffer.at[k],
                send_sem=send.at[k], recv_sem=recv.at[k],
                device_id=peer(k), device_id_type=MESH,
            )
            for k in range(1, count)
        ]
        for copy in copies:
            copy.start()
        return copies

    lat_copies = exchange(sums_lat, tile, nl, lat_send, lat_recv, lambda k: at(k, 0))

    for w in range(wins):
        for rows, spread in levels(w):
            for c, lanes in chunks:
                stage[c, spread] = grad_s[rows, lanes]

    def quadrant(q):
        cells = [stage[c, pl.ds(q * quad, quad)] for c, _ in chunks]
        return jnp.concatenate(cells, axis=1).reshape(back_out.shape[1:])

    returns = []
    for q in (3, 2, 1):
        back_out[q - 1] = quadrant(q).astype(BF16)
        returns.append(pltpu.make_async_remote_copy(
            src_ref=back_out.at[q - 1], dst_ref=back_in.at[q - 1],
            send_sem=bsend_sem.at[q - 1], recv_sem=brecv_sem.at[q - 1],
            device_id=at(q // 2, q % 2), device_id_type=MESH,
        ))
        returns[-1].start()

    for copy in lat_copies:
        copy.wait()
    lat_sum = jnp.sum(sums_lat[...], axis=0)
    lon_copies = exchange(sums_lon, lat_sum, nn, lon_send, lon_recv, lambda k: at(0, k))
    for move in returns:
        move.wait()
    for copy in lon_copies:
        copy.wait()
    total = jnp.sum(jnp.sum(sums_lon[...], axis=0), keepdims=True)
    entries = wins * size * width * nl * nn
    clip = jnp.minimum(1.0, CLIP_LEVEL * lax.rsqrt(total / entries + 1e-06))

    out_ref[lay.source(0)] = (quadrant(0) * clip.reshape(1, 1, 1, 1)).astype(BF16)
    for q in range(1, 4):
        out_ref[lay.source(q)] = (back_in[q - 1].astype(F32) * clip.reshape(1, 1, 1, 1)).astype(BF16)


def solution(mesh):
    n_lat, n_lon = mesh.shape["lat"], mesh.shape["lon"]

    def shards(
        latent, cotangent, band_ids, attn_gain, attn_bias, ffn_gain, ffn_bias,
        attn_weight, out_weight, up_weight, down_weight,
    ):
        latent, cotangent = (a.transpose(1, 2, 0, 3) for a in (latent, cotangent))
        lay = Layout(latent.shape, n_lat, n_lon)
        quadrant = (lay.hr, lay.hc, lay.levels, lay.width)
        width, tokens = lay.width, lay.wins * lay.size
        hbm = pl.BlockSpec(memory_space=pltpu.HBM)
        vmem = pl.BlockSpec(memory_space=pltpu.VMEM)
        dma = pltpu.SemaphoreType.DMA
        scratch = [
            pltpu.SMEM(band_ids.shape, jnp.int32),
            pltpu.VMEM((1, width), F32), pltpu.VMEM((1, width), F32),
            pltpu.VMEM((1, width), F32), pltpu.VMEM((1, width), F32),
            pltpu.VMEM(attn_weight.shape, BF16), pltpu.VMEM(out_weight.shape, BF16),
            pltpu.VMEM(up_weight.shape, BF16), pltpu.VMEM(down_weight.shape, BF16),
            pltpu.VMEM((2, 4) + quadrant, BF16),
            pltpu.VMEM((width // 128, tokens, 128), F32),
            pltpu.VMEM((tokens, width), F32),
            pltpu.VMEM((tokens, width), F32),
            pltpu.VMEM((tokens, width), F32),
            pltpu.VMEM((lay.wins, lay.size, lay.size), F32),
            pltpu.VMEM((lay.wins, 3 * width, lay.size), BF16),
            pltpu.VMEM((lay.wins * HEADS, lay.size, lay.size), F32),
            pltpu.VMEM((lay.wins, width, lay.size), F32),
            pltpu.VMEM((lay.wins, width, lay.size), BF16),
            pltpu.VMEM((lay.wins, 3 * width, lay.size), BF16),
            pltpu.VMEM((tokens, width), F32),
            pltpu.VMEM((3,) + quadrant, BF16),
            pltpu.VMEM((3,) + quadrant, BF16),
            pltpu.VMEM((n_lat, 8, 128), F32),
            pltpu.VMEM((n_lon, 8, 128), F32),
            dma((9,)), dma((2,)), dma((2, 4)), dma((2, 4)), dma((3,)), dma((3,)),
            dma((n_lat,)), dma((n_lat,)), dma((n_lon,)), dma((n_lon,)),
        ]
        return pl.pallas_call(
            functools.partial(kernel, lay),
            out_shape=jax.ShapeDtypeStruct(latent.shape, BF16),
            in_specs=[hbm] * 11,
            out_specs=vmem,
            scratch_shapes=scratch,
            compiler_params=pltpu.CompilerParams(
                collective_id=0, has_side_effects=True, vmem_limit_bytes=63 * 2**20
            ),
        )(
            latent, cotangent, band_ids,
            attn_gain.reshape(1, width), attn_bias.reshape(1, width),
            ffn_gain.reshape(1, width), ffn_bias.reshape(1, width),
            attn_weight, out_weight, up_weight, down_weight,
        ).transpose(2, 0, 1, 3)

    block = P(None, "lat", "lon", None)
    return jax.shard_map(
        shards, mesh=mesh, in_specs=(block, block) + (P(),) * 9, out_specs=block, check_vma=False
    )
```

```python
import functools

import jax
import jax.numpy as jnp
from jax import lax
from jax.experimental import pallas as pl
from jax.experimental.pallas import tpu as pltpu
from jax.sharding import PartitionSpec as P

HEADS = 16
WIN_LEV = 2
WIN_LAT = 6
WIN_LON = 12

SQRT_HALF = 0.7071067811865476
INV_SQRT_TAU = 0.3989422804014327
LOG2_E = 1.4426950408889634
CLIP_LEVEL = 0.2
MESH = pl.DeviceIdType.MESH
F32 = jnp.float32
BF16 = jnp.bfloat16


def dot(a, b, dims=((1,), (0,))):
    return lax.dot_general(a, b, (dims, ((), ())), preferred_element_type=F32)


def normalize(values):
    center = values - jnp.mean(values, axis=-1, keepdims=True)
    inv_scale = lax.rsqrt(jnp.mean(center * center, axis=-1, keepdims=True) + 1e-05)
    return center * inv_scale, inv_scale


def norm_back(normed, inv_scale, gain, grad_norm):
    scaled = grad_norm * gain
    return inv_scale * (
        scaled
        - jnp.mean(scaled, axis=-1, keepdims=True)
        - normed * jnp.mean(scaled * normed, axis=-1, keepdims=True)
    )


class Layout:
    def __init__(self, shape, n_lat, n_lon):
        self.rows, self.cols, self.levels, self.width = shape
        assert self.rows == WIN_LAT and self.cols == WIN_LON
        self.n_lat, self.n_lon = n_lat, n_lon
        self.hr, self.hc = self.rows // 2, self.cols // 2
        self.wins = self.levels // WIN_LEV
        self.plane = self.rows * self.cols
        self.size = WIN_LEV * self.plane
        self.quad = self.plane // 4 * self.levels

    def source(self, q):
        row, col = (0 if q // 2 else self.hr), (0 if q % 2 else self.hc)
        return pl.ds(row, self.hr), pl.ds(col, self.hc)


def mask_bias(lay, window, band_ref, row_start):
    total = band_ref.shape[0]
    bands = [band_ref[lax.rem(row_start + r + lay.hr, total)] for r in range(lay.rows)]

    def labels(dim):
        cell = lax.broadcasted_iota(jnp.int32, (lay.size, lay.size), dim)
        level = jnp.zeros_like(cell)
        for i in range(1, WIN_LEV):
            level += (cell >= i * lay.plane).astype(jnp.int32)
        cell = cell - level * lay.plane
        half = (cell >= lay.plane // 2).astype(jnp.int32)
        cell = cell - half * (lay.plane // 2)
        cell = cell - (cell >= lay.plane // 4).astype(jnp.int32) * (lay.plane // 4)
        row = half * lay.hr
        for i in range(1, lay.hr):
            row += (cell >= i * lay.hc).astype(jnp.int32)
        label = jnp.zeros_like(cell)
        for r in range(lay.rows):
            label = jnp.where(row == r, 2 * bands[r], label)
        last = level + window * WIN_LEV == lay.levels - 1
        return label + last.astype(jnp.int32)

    return jnp.where(labels(0) == labels(1), 0.0, -jnp.inf).astype(F32)


def kernel(
    lay,
    latent_hbm, cotangent_hbm, band_hbm, ag_hbm, ab_hbm, fg_hbm, fb_hbm,
    wqkv_hbm, wout_hbm, wup_hbm, wdown_hbm,
    out_ref,
    band_ref, ag_ref, ab_ref, fg_ref, fb_ref, wqkv, wout, wup, wdown,
    landed, stage, xs, cs, n1_s, bias, qkv_t, terms, inv_s, mix_t, gm_t, gqkv_t,
    grad_s, back_out, back_in, sums_lat, sums_lon,
    load_sem, own_sem, send_sem, recv_sem, bsend_sem, brecv_sem,
    lat_send, lat_recv, lon_send, lon_recv,
):
    lat, lon = lax.axis_index("lat"), lax.axis_index("lon")
    nl, nn = lay.n_lat, lay.n_lon
    width, quad, size, wins = lay.width, lay.quad, lay.size, lay.wins
    head = width // HEADS

    def at(dlat, dlon):
        return {"lat": lax.rem(lat + dlat + nl, nl), "lon": lax.rem(lon + dlon + nn, nn)}

    barrier = pltpu.get_barrier_semaphore()
    peers = [at(k, 0) for k in range(1, nl)] + [at(0, k) for k in range(1, nn)]
    peers += [at(1, 1), at(-1, -1)]
    for peer in peers:
        pl.semaphore_signal(barrier, inc=1, device_id=peer, device_id_type=MESH)

    blocks = (latent_hbm, cotangent_hbm)
    owns = [
        pltpu.make_async_copy(block.at[lay.source(0)], landed.at[i, 0], own_sem.at[i])
        for i, block in enumerate(blocks)
    ]
    loads = [
        pltpu.make_async_copy(src, dst, load_sem.at[i])
        for i, (src, dst) in enumerate([
            (band_hbm, band_ref), (ag_hbm, ag_ref), (ab_hbm, ab_ref), (wqkv_hbm, wqkv),
            (wdown_hbm, wdown), (wout_hbm, wout), (wup_hbm, wup), (fg_hbm, fg_ref), (fb_hbm, fb_ref),
        ])
    ]
    for load in owns + loads:
        load.start()

    pl.semaphore_wait(barrier, len(peers))
    moves = [
        pltpu.make_async_remote_copy(
            src_ref=block.at[lay.source(q)], dst_ref=landed.at[i, q],
            send_sem=send_sem.at[i, q], recv_sem=recv_sem.at[i, q],
            device_id=at(-(q // 2), -(q % 2)), device_id_type=MESH,
        )
        for i, block in enumerate(blocks)
        for q in (3, 2, 1)
    ]
    for move in moves[:3]:
        move.start()

    loads[0].wait()
    for w in range(wins):
        bias[w] = mask_bias(lay, w, band_ref, lat * lay.rows)

    chunks = [(c, slice(c * 128, (c + 1) * 128)) for c in range(width // 128)]

    def levels(w):
        for lev in range(WIN_LEV):
            level = (w * WIN_LEV + lev + 1) % lay.levels
            rows = pl.ds((w * WIN_LEV + lev) * lay.plane, lay.plane)
            yield rows, pl.ds(level, lay.plane, stride=lay.levels)

    def take(i, kept):
        owns[i].wait()
        for move in moves[3 * i : 3 * i + 3]:
            move.wait()
        for q in range(4):
            cells = landed[i, q].astype(F32).reshape(quad, width)
            for c, lanes in chunks:
                stage[c, pl.ds(q * quad, quad)] = cells[:, lanes]
        for w in range(wins):
            for rows, spread in levels(w):
                for c, lanes in chunks:
                    kept[rows, lanes] = stage[c, spread]

    take(0, xs)
    for move in moves[3:]:
        move.start()

    loads[1].wait()
    loads[2].wait()
    n1, r1 = normalize(xs[...])
    n1_s[...] = n1
    h1 = (n1 * ag_ref[...] + ab_ref[...]).astype(BF16)
    loads[3].wait()
    for c in range(3):
        columns = slice(c * width, (c + 1) * width)
        qkv = dot(h1, wqkv[:, columns])
        for w in range(wins):
            qkv_t[w, columns] = qkv[w * size : (w + 1) * size].T.astype(BF16)

    scale = head ** (-0.5)
    unroll = 16

    def parts_of(w, h):
        def rows(block):
            return pl.ds(pl.multiple_of(block * width + h * head, head), head)

        return [qkv_t[w, rows(b)] for b in range(3)]

    def ahead(step, carry):
        for u in range(unroll):
            h = step * unroll + u
            for w in range(wins):
                q_t, k_t, v_t = parts_of(w, h)
                scores = dot(k_t, q_t, ((0,), (0,))) + bias[w]
                top = jnp.max(scores, axis=0, keepdims=True)
                expo = jnp.exp2((scores - top) * (scale * LOG2_E))
                inv = 1.0 / jnp.sum(expo, axis=0, keepdims=True)
                expo = expo.astype(BF16)
                terms[h * wins + w] = expo
                inv_s[h * wins + w] = inv
                mix_t[w, pl.ds(pl.multiple_of(h * head, head), head)] = dot(v_t, expo) * inv
        return carry

    lax.fori_loop(0, HEADS // unroll, ahead, 0)

    for load in loads[4:]:
        load.wait()
    mixed = jnp.concatenate([mix_t[w].T.astype(BF16) for w in range(wins)], axis=0)
    resid = xs[...] + dot(mixed, wout[...])

    take(1, cs)
    n2, r2 = normalize(resid)
    h2 = (n2 * fg_ref[...] + fb_ref[...]).astype(BF16)
    cot = cs[...].astype(BF16)
    hidden = wup.shape[1]
    chunk = min(256, hidden)
    grad_h2 = None
    for c in range(0, hidden, chunk):
        pre = dot(h2, wup[:, c : c + chunk])
        act = dot(cot, wdown[c : c + chunk], ((1,), (1,)))
        slope = 0.5 * (1.0 + lax.erf(pre * SQRT_HALF)) + pre * jnp.exp(-0.5 * pre * pre) * INV_SQRT_TAU
        grad_pre = (act * slope).astype(BF16)
        term = dot(grad_pre, wup[:, c : c + chunk], ((1,), (1,)))
        grad_h2 = term if grad_h2 is None else grad_h2 + term
    grad_resid = cs[...] + norm_back(n2, r2, fg_ref[...], grad_h2)
    grad_s[...] = grad_resid
    grad_r = grad_resid.astype(BF16)
    for w in range(wins):
        gm_t[w] = dot(wout[...], grad_r[w * size : (w + 1) * size], ((1,), (1,)))

    def behind(step, carry):
        for u in range(unroll):
            h = step * unroll + u
            mine = pl.ds(pl.multiple_of(h * head, head), head)
            for w in range(wins):
                q_t, k_t, v_t = parts_of(w, h)
                g_t = gm_t[w, mine] * inv_s[h * wins + w]
                expo = terms[h * wins + w]
                inner = jnp.sum(mix_t[w, mine] * g_t, axis=0, keepdims=True)
                g_t = g_t.astype(BF16)
                grad_p = dot(v_t, g_t, ((0,), (0,)))
                grad_sc = expo * (grad_p - inner).astype(BF16)
                grads = (
                    dot(k_t, grad_sc) * scale,
                    dot(q_t, grad_sc, ((1,), (1,))) * scale,
                    dot(g_t, expo, ((1,), (1,))),
                )
                for b in range(3):
                    rows = pl.ds(pl.multiple_of(b * width + h * head, head), head)
                    gqkv_t[w, rows] = grads[b].astype(BF16)
        return carry

    lax.fori_loop(0, HEADS // unroll, behind, 0)

    grad_h1 = jnp.concatenate([dot(wqkv[...], gqkv_t[w]).T for w in range(wins)], axis=0)
    grad = grad_s[...] + norm_back(n1_s[...], r1, ag_ref[...], grad_h1)
    grad_s[...] = grad

    squares = jnp.sum((grad * grad).reshape(-1, 8, width), axis=0)
    tile = functools.reduce(jnp.add, [squares[:, c : c + 128] for c in range(0, width, 128)])

    def exchange(buffer, own, count, send, recv, peer):
        buffer[0] = own
        copies = [
            pltpu.make_async_remote_copy(
                src_ref=buffer.at[0], dst_ref=buffer.at[k],
                send_sem=send.at[k], recv_sem=recv.at[k],
                device_id=peer(k), device_id_type=MESH,
            )
            for k in range(1, count)
        ]
        for copy in copies:
            copy.start()
        return copies

    lat_copies = exchange(sums_lat, tile, nl, lat_send, lat_recv, lambda k: at(k, 0))

    for w in range(wins):
        for rows, spread in levels(w):
            for c, lanes in chunks:
                stage[c, spread] = grad_s[rows, lanes]

    def quadrant(q):
        cells = [stage[c, pl.ds(q * quad, quad)] for c, _ in chunks]
        return jnp.concatenate(cells, axis=1).reshape(back_out.shape[1:])

    returns = []
    for q in (3, 2, 1):
        back_out[q - 1] = quadrant(q).astype(BF16)
        returns.append(pltpu.make_async_remote_copy(
            src_ref=back_out.at[q - 1], dst_ref=back_in.at[q - 1],
            send_sem=bsend_sem.at[q - 1], recv_sem=brecv_sem.at[q - 1],
            device_id=at(q // 2, q % 2), device_id_type=MESH,
        ))
        returns[-1].start()

    for copy in lat_copies:
        copy.wait()
    lat_sum = jnp.sum(sums_lat[...], axis=0)
    lon_copies = exchange(sums_lon, lat_sum, nn, lon_send, lon_recv, lambda k: at(0, k))
    for move in returns:
        move.wait()
    for copy in lon_copies:
        copy.wait()
    total = jnp.sum(jnp.sum(sums_lon[...], axis=0), keepdims=True)
    entries = wins * size * width * nl * nn
    clip = jnp.minimum(1.0, CLIP_LEVEL * lax.rsqrt(total / entries + 1e-06))

    out_ref[lay.source(0)] = (quadrant(0) * clip.reshape(1, 1, 1, 1)).astype(BF16)
    for q in range(1, 4):
        out_ref[lay.source(q)] = (back_in[q - 1].astype(F32) * clip.reshape(1, 1, 1, 1)).astype(BF16)


def solution(mesh):
    n_lat, n_lon = mesh.shape["lat"], mesh.shape["lon"]

    def shards(
        latent, cotangent, band_ids, attn_gain, attn_bias, ffn_gain, ffn_bias,
        attn_weight, out_weight, up_weight, down_weight,
    ):
        latent, cotangent = (a.transpose(1, 2, 0, 3) for a in (latent, cotangent))
        lay = Layout(latent.shape, n_lat, n_lon)
        quadrant = (lay.hr, lay.hc, lay.levels, lay.width)
        width, tokens = lay.width, lay.wins * lay.size
        hbm = pl.BlockSpec(memory_space=pltpu.HBM)
        vmem = pl.BlockSpec(memory_space=pltpu.VMEM)
        dma = pltpu.SemaphoreType.DMA
        scratch = [
            pltpu.SMEM(band_ids.shape, jnp.int32),
            pltpu.VMEM((1, width), F32), pltpu.VMEM((1, width), F32),
            pltpu.VMEM((1, width), F32), pltpu.VMEM((1, width), F32),
            pltpu.VMEM(attn_weight.shape, BF16), pltpu.VMEM(out_weight.shape, BF16),
            pltpu.VMEM(up_weight.shape, BF16), pltpu.VMEM(down_weight.shape, BF16),
            pltpu.VMEM((2, 4) + quadrant, BF16),
            pltpu.VMEM((width // 128, tokens, 128), F32),
            pltpu.VMEM((tokens, width), F32),
            pltpu.VMEM((tokens, width), F32),
            pltpu.VMEM((tokens, width), F32),
            pltpu.VMEM((lay.wins, lay.size, lay.size), F32),
            pltpu.VMEM((lay.wins, 3 * width, lay.size), BF16),
            pltpu.VMEM((lay.wins * HEADS, lay.size, lay.size), BF16),
            pltpu.VMEM((lay.wins * HEADS, 1, lay.size), F32),
            pltpu.VMEM((lay.wins, width, lay.size), F32),
            pltpu.VMEM((lay.wins, width, lay.size), F32),
            pltpu.VMEM((lay.wins, 3 * width, lay.size), BF16),
            pltpu.VMEM((tokens, width), F32),
            pltpu.VMEM((3,) + quadrant, BF16),
            pltpu.VMEM((3,) + quadrant, BF16),
            pltpu.VMEM((n_lat, 8, 128), F32),
            pltpu.VMEM((n_lon, 8, 128), F32),
            dma((9,)), dma((2,)), dma((2, 4)), dma((2, 4)), dma((3,)), dma((3,)),
            dma((n_lat,)), dma((n_lat,)), dma((n_lon,)), dma((n_lon,)),
        ]
        return pl.pallas_call(
            functools.partial(kernel, lay),
            out_shape=jax.ShapeDtypeStruct(latent.shape, BF16),
            in_specs=[hbm] * 11,
            out_specs=vmem,
            scratch_shapes=scratch,
            compiler_params=pltpu.CompilerParams(
                collective_id=0, has_side_effects=True, vmem_limit_bytes=63 * 2**20
            ),
        )(
            latent, cotangent, band_ids,
            attn_gain.reshape(1, width), attn_bias.reshape(1, width),
            ffn_gain.reshape(1, width), ffn_bias.reshape(1, width),
            attn_weight, out_weight, up_weight, down_weight,
        ).transpose(2, 0, 1, 3)

    block = P(None, "lat", "lon", None)
    return jax.shard_map(
        shards, mesh=mesh, in_specs=(block, block) + (P(),) * 9, out_specs=block, check_vma=False
    )
```

```python
import functools

import jax
import jax.numpy as jnp
from jax import lax
from jax.experimental import pallas as pl
from jax.experimental.pallas import tpu as pltpu
from jax.sharding import PartitionSpec as P

HEADS = 16
WIN_LEV = 2
WIN_LAT = 6
WIN_LON = 12

SQRT_HALF = 0.7071067811865476
INV_SQRT_TAU = 0.3989422804014327
LOG2_E = 1.4426950408889634
CLIP_LEVEL = 0.2
MESH = pl.DeviceIdType.MESH
F32 = jnp.float32
BF16 = jnp.bfloat16


def dot(a, b, dims=((1,), (0,))):
    return lax.dot_general(a, b, (dims, ((), ())), preferred_element_type=F32)


def normalize(values):
    center = values - jnp.mean(values, axis=-1, keepdims=True)
    inv_scale = lax.rsqrt(jnp.mean(center * center, axis=-1, keepdims=True) + 1e-05)
    return center * inv_scale, inv_scale


def norm_back(normed, inv_scale, gain, grad_norm):
    scaled = grad_norm * gain
    return inv_scale * (
        scaled
        - jnp.mean(scaled, axis=-1, keepdims=True)
        - normed * jnp.mean(scaled * normed, axis=-1, keepdims=True)
    )


class Layout:
    def __init__(self, shape, n_lat, n_lon):
        self.rows, self.cols, self.levels, self.width = shape
        assert self.rows == WIN_LAT and self.cols == WIN_LON
        self.n_lat, self.n_lon = n_lat, n_lon
        self.hr, self.hc = self.rows // 2, self.cols // 2
        self.wins = self.levels // WIN_LEV
        self.plane = self.rows * self.cols
        self.size = WIN_LEV * self.plane
        self.quad = self.plane // 4 * self.levels

    def source(self, q):
        row, col = (0 if q // 2 else self.hr), (0 if q % 2 else self.hc)
        return pl.ds(row, self.hr), pl.ds(col, self.hc)


def mask_bias(lay, window, band_ref, row_start):
    total = band_ref.shape[0]
    bands = [band_ref[lax.rem(row_start + r + lay.hr, total)] for r in range(lay.rows)]

    def labels(dim):
        cell = lax.broadcasted_iota(jnp.int32, (lay.size, lay.size), dim)
        level = jnp.zeros_like(cell)
        for i in range(1, WIN_LEV):
            level += (cell >= i * lay.plane).astype(jnp.int32)
        cell = cell - level * lay.plane
        half = (cell >= lay.plane // 2).astype(jnp.int32)
        cell = cell - half * (lay.plane // 2)
        cell = cell - (cell >= lay.plane // 4).astype(jnp.int32) * (lay.plane // 4)
        row = half * lay.hr
        for i in range(1, lay.hr):
            row += (cell >= i * lay.hc).astype(jnp.int32)
        label = jnp.zeros_like(cell)
        for r in range(lay.rows):
            label = jnp.where(row == r, 2 * bands[r], label)
        last = level + window * WIN_LEV == lay.levels - 1
        return label + last.astype(jnp.int32)

    return jnp.where(labels(0) == labels(1), 0.0, -jnp.inf).astype(F32)


def kernel(
    lay,
    latent_hbm, cotangent_hbm, band_hbm, ag_hbm, ab_hbm, fg_hbm, fb_hbm,
    wqkv_hbm, wout_hbm, wup_hbm, wdown_hbm,
    out_ref,
    band_ref, ag_ref, ab_ref, fg_ref, fb_ref, wqkv, wout, wup, wdown,
    landed, stage, xs, cs, n1_s, bias, qkv_t, kv_s, terms, inv_s, mix_t, gm_t, gqkv_t,
    grad_s, back_out, back_in, sums_lat, sums_lon,
    load_sem, own_sem, send_sem, recv_sem, bsend_sem, brecv_sem,
    lat_send, lat_recv, lon_send, lon_recv,
):
    lat, lon = lax.axis_index("lat"), lax.axis_index("lon")
    nl, nn = lay.n_lat, lay.n_lon
    width, quad, size, wins = lay.width, lay.quad, lay.size, lay.wins
    head = width // HEADS

    def at(dlat, dlon):
        return {"lat": lax.rem(lat + dlat + nl, nl), "lon": lax.rem(lon + dlon + nn, nn)}

    barrier = pltpu.get_barrier_semaphore()
    peers = [at(k, 0) for k in range(1, nl)] + [at(0, k) for k in range(1, nn)]
    peers += [at(1, 1), at(-1, -1)]
    for peer in peers:
        pl.semaphore_signal(barrier, inc=1, device_id=peer, device_id_type=MESH)

    blocks = (latent_hbm, cotangent_hbm)
    owns = [
        pltpu.make_async_copy(block.at[lay.source(0)], landed.at[i, 0], own_sem.at[i])
        for i, block in enumerate(blocks)
    ]
    loads = [
        pltpu.make_async_copy(src, dst, load_sem.at[i])
        for i, (src, dst) in enumerate([
            (band_hbm, band_ref), (ag_hbm, ag_ref), (ab_hbm, ab_ref), (wqkv_hbm, wqkv),
            (wdown_hbm, wdown), (wout_hbm, wout), (wup_hbm, wup), (fg_hbm, fg_ref), (fb_hbm, fb_ref),
        ])
    ]
    for load in owns + loads:
        load.start()

    pl.semaphore_wait(barrier, len(peers))
    moves = [
        pltpu.make_async_remote_copy(
            src_ref=block.at[lay.source(q)], dst_ref=landed.at[i, q],
            send_sem=send_sem.at[i, q], recv_sem=recv_sem.at[i, q],
            device_id=at(-(q // 2), -(q % 2)), device_id_type=MESH,
        )
        for i, block in enumerate(blocks)
        for q in (3, 2, 1)
    ]
    for move in moves[:3]:
        move.start()

    loads[0].wait()
    for w in range(wins):
        bias[w] = mask_bias(lay, w, band_ref, lat * lay.rows)

    chunks = [(c, slice(c * 128, (c + 1) * 128)) for c in range(width // 128)]

    def levels(w):
        for lev in range(WIN_LEV):
            level = (w * WIN_LEV + lev + 1) % lay.levels
            rows = pl.ds((w * WIN_LEV + lev) * lay.plane, lay.plane)
            yield rows, pl.ds(level, lay.plane, stride=lay.levels)

    def take(i, kept):
        owns[i].wait()
        for move in moves[3 * i : 3 * i + 3]:
            move.wait()
        for q in range(4):
            cells = landed[i, q].astype(F32).reshape(quad, width)
            for c, lanes in chunks:
                stage[c, pl.ds(q * quad, quad)] = cells[:, lanes]
        for w in range(wins):
            for rows, spread in levels(w):
                for c, lanes in chunks:
                    kept[rows, lanes] = stage[c, spread]

    take(0, xs)
    for move in moves[3:]:
        move.start()

    loads[1].wait()
    loads[2].wait()
    n1, r1 = normalize(xs[...])
    n1_s[...] = n1
    h1 = (n1 * ag_ref[...] + ab_ref[...]).astype(BF16)
    loads[3].wait()
    for c in range(3):
        columns = slice(c * width, (c + 1) * width)
        qkv = dot(h1, wqkv[:, columns])
        for w in range(wins):
            cells = qkv[w * size : (w + 1) * size]
            qkv_t[w, columns] = cells.T.astype(BF16)
            if c:
                kv_s[c - 1, w] = cells.astype(BF16)

    scale = head ** (-0.5)
    group = 128 // head

    def parts_of(w, h):
        return [qkv_t[w, pl.ds(b * width + h * head, head)] for b in range(3)]

    def against(which, w, h, part):
        zero = jnp.zeros_like(part)
        spread = [part if i == h % group else zero for i in range(group)]
        lanes = pl.ds(h // group * 128, 128)
        return dot(kv_s[which, w, :, lanes], jnp.concatenate(spread, axis=0))

    for h in range(HEADS):
        for w in range(wins):
            q_t, _, v_t = parts_of(w, h)
            scores = against(0, w, h, q_t) + bias[w]
            top = jnp.max(scores, axis=0, keepdims=True)
            expo = jnp.exp2((scores - top) * (scale * LOG2_E))
            inv = 1.0 / jnp.sum(expo, axis=0, keepdims=True)
            expo = expo.astype(BF16)
            terms[h * wins + w] = expo
            inv_s[h * wins + w] = inv
            mix_t[w, pl.ds(h * head, head)] = dot(v_t, expo) * inv

    for load in loads[4:]:
        load.wait()
    mixed = jnp.concatenate([mix_t[w].T.astype(BF16) for w in range(wins)], axis=0)
    resid = xs[...] + dot(mixed, wout[...])

    take(1, cs)
    n2, r2 = normalize(resid)
    h2 = (n2 * fg_ref[...] + fb_ref[...]).astype(BF16)
    cot = cs[...].astype(BF16)
    hidden = wup.shape[1]
    chunk = min(512, hidden)
    grad_h2 = None
    for c in range(0, hidden, chunk):
        pre = dot(h2, wup[:, c : c + chunk])
        act = dot(cot, wdown[c : c + chunk], ((1,), (1,)))
        slope = 0.5 * (1.0 + lax.erf(pre * SQRT_HALF)) + pre * jnp.exp(-0.5 * pre * pre) * INV_SQRT_TAU
        grad_pre = (act * slope).astype(BF16)
        term = dot(grad_pre, wup[:, c : c + chunk], ((1,), (1,)))
        grad_h2 = term if grad_h2 is None else grad_h2 + term
    grad_resid = cs[...] + norm_back(n2, r2, fg_ref[...], grad_h2)
    grad_s[...] = grad_resid
    grad_r = grad_resid.astype(BF16)
    for w in range(wins):
        gm_t[w] = dot(wout[...], grad_r[w * size : (w + 1) * size], ((1,), (1,)))

    for h in range(HEADS):
        mine = pl.ds(h * head, head)
        for w in range(wins):
            q_t, k_t, _ = parts_of(w, h)
            g_t = gm_t[w, mine] * inv_s[h * wins + w]
            expo = terms[h * wins + w]
            inner = jnp.sum(mix_t[w, mine] * g_t, axis=0, keepdims=True)
            g_t = g_t.astype(BF16)
            grad_sc = expo * (against(1, w, h, g_t) - inner).astype(BF16)
            grads = (
                dot(k_t, grad_sc) * scale,
                dot(q_t, grad_sc, ((1,), (1,))) * scale,
                dot(g_t, expo, ((1,), (1,))),
            )
            for b in range(3):
                gqkv_t[w, pl.ds(b * width + h * head, head)] = grads[b].astype(BF16)

    grad_h1 = jnp.concatenate([dot(wqkv[...], gqkv_t[w]).T for w in range(wins)], axis=0)
    grad = grad_s[...] + norm_back(n1_s[...], r1, ag_ref[...], grad_h1)
    grad_s[...] = grad

    squares = jnp.sum((grad * grad).reshape(-1, 8, width), axis=0)
    tile = functools.reduce(jnp.add, [squares[:, c : c + 128] for c in range(0, width, 128)])

    def exchange(buffer, own, count, send, recv, peer):
        buffer[0] = own
        copies = [
            pltpu.make_async_remote_copy(
                src_ref=buffer.at[0], dst_ref=buffer.at[k],
                send_sem=send.at[k], recv_sem=recv.at[k],
                device_id=peer(k), device_id_type=MESH,
            )
            for k in range(1, count)
        ]
        for copy in copies:
            copy.start()
        return copies

    lat_copies = exchange(sums_lat, tile, nl, lat_send, lat_recv, lambda k: at(k, 0))

    for w in range(wins):
        for rows, spread in levels(w):
            for c, lanes in chunks:
                stage[c, spread] = grad_s[rows, lanes]

    def quadrant(q):
        cells = [stage[c, pl.ds(q * quad, quad)] for c, _ in chunks]
        return jnp.concatenate(cells, axis=1).reshape(back_out.shape[1:])

    returns = []
    for q in (3, 2, 1):
        back_out[q - 1] = quadrant(q).astype(BF16)
        returns.append(pltpu.make_async_remote_copy(
            src_ref=back_out.at[q - 1], dst_ref=back_in.at[q - 1],
            send_sem=bsend_sem.at[q - 1], recv_sem=brecv_sem.at[q - 1],
            device_id=at(q // 2, q % 2), device_id_type=MESH,
        ))
        returns[-1].start()

    for copy in lat_copies:
        copy.wait()
    lat_sum = jnp.sum(sums_lat[...], axis=0)
    lon_copies = exchange(sums_lon, lat_sum, nn, lon_send, lon_recv, lambda k: at(0, k))
    for move in returns:
        move.wait()
    for copy in lon_copies:
        copy.wait()
    total = jnp.sum(jnp.sum(sums_lon[...], axis=0), keepdims=True)
    entries = wins * size * width * nl * nn
    clip = jnp.minimum(1.0, CLIP_LEVEL * lax.rsqrt(total / entries + 1e-06))

    out_ref[lay.source(0)] = (quadrant(0) * clip.reshape(1, 1, 1, 1)).astype(BF16)
    for q in range(1, 4):
        out_ref[lay.source(q)] = (back_in[q - 1].astype(F32) * clip.reshape(1, 1, 1, 1)).astype(BF16)


def solution(mesh):
    n_lat, n_lon = mesh.shape["lat"], mesh.shape["lon"]

    def shards(
        latent, cotangent, band_ids, attn_gain, attn_bias, ffn_gain, ffn_bias,
        attn_weight, out_weight, up_weight, down_weight,
    ):
        latent, cotangent = (a.transpose(1, 2, 0, 3) for a in (latent, cotangent))
        lay = Layout(latent.shape, n_lat, n_lon)
        quadrant = (lay.hr, lay.hc, lay.levels, lay.width)
        width, tokens = lay.width, lay.wins * lay.size
        hbm = pl.BlockSpec(memory_space=pltpu.HBM)
        vmem = pl.BlockSpec(memory_space=pltpu.VMEM)
        dma = pltpu.SemaphoreType.DMA
        scratch = [
            pltpu.SMEM(band_ids.shape, jnp.int32),
            pltpu.VMEM((1, width), F32), pltpu.VMEM((1, width), F32),
            pltpu.VMEM((1, width), F32), pltpu.VMEM((1, width), F32),
            pltpu.VMEM(attn_weight.shape, BF16), pltpu.VMEM(out_weight.shape, BF16),
            pltpu.VMEM(up_weight.shape, BF16), pltpu.VMEM(down_weight.shape, BF16),
            pltpu.VMEM((2, 4) + quadrant, BF16),
            pltpu.VMEM((width // 128, tokens, 128), F32),
            pltpu.VMEM((tokens, width), F32),
            pltpu.VMEM((tokens, width), F32),
            pltpu.VMEM((tokens, width), F32),
            pltpu.VMEM((lay.wins, lay.size, lay.size), F32),
            pltpu.VMEM((lay.wins, 3 * width, lay.size), BF16),
            pltpu.VMEM((2, lay.wins, lay.size, width), BF16),
            pltpu.VMEM((lay.wins * HEADS, lay.size, lay.size), BF16),
            pltpu.VMEM((lay.wins * HEADS, 1, lay.size), F32),
            pltpu.VMEM((lay.wins, width, lay.size), F32),
            pltpu.VMEM((lay.wins, width, lay.size), F32),
            pltpu.VMEM((lay.wins, 3 * width, lay.size), BF16),
            pltpu.VMEM((tokens, width), F32),
            pltpu.VMEM((3,) + quadrant, BF16),
            pltpu.VMEM((3,) + quadrant, BF16),
            pltpu.VMEM((n_lat, 8, 128), F32),
            pltpu.VMEM((n_lon, 8, 128), F32),
            dma((9,)), dma((2,)), dma((2, 4)), dma((2, 4)), dma((3,)), dma((3,)),
            dma((n_lat,)), dma((n_lat,)), dma((n_lon,)), dma((n_lon,)),
        ]
        return pl.pallas_call(
            functools.partial(kernel, lay),
            out_shape=jax.ShapeDtypeStruct(latent.shape, BF16),
            in_specs=[hbm] * 11,
            out_specs=vmem,
            scratch_shapes=scratch,
            compiler_params=pltpu.CompilerParams(
                collective_id=0, has_side_effects=True, vmem_limit_bytes=63 * 2**20
            ),
        )(
            latent, cotangent, band_ids,
            attn_gain.reshape(1, width), attn_bias.reshape(1, width),
            ffn_gain.reshape(1, width), ffn_bias.reshape(1, width),
            attn_weight, out_weight, up_weight, down_weight,
        ).transpose(2, 0, 1, 3)

    block = P(None, "lat", "lon", None)
    return jax.shard_map(
        shards, mesh=mesh, in_specs=(block, block) + (P(),) * 9, out_specs=block, check_vma=False
    )
```
